512 devices in a mesh: rep: 32 (over z, x_lo, core), fsdp: 16 (over x_hi, y).
Axes of the slice: x: 4 (x_hi: 2, x_lo: 2; x = x_hi * 2 + x_lo), y: 8, z: 8, core: 2. Of those that a mesh axis runs over, the one named last changes fastest.
Arguments:
- acts: bfloat16 [65536, 64], P(('rep', 'fsdp')), may hold values from -16 to 16
- cotangent: bfloat16 [65536, 14336], P(('rep', 'fsdp')), may hold values from -0.125 to 0.125
- weight: float32 [64, 14336], P('fsdp'), may hold values from -0.0625 to 0.0625
- momentum: float32 [32, 64, 14336], P('rep', 'fsdp'), may hold values from -6 to 6
- bands: int32 [64, 4], P('fsdp'), may hold values from 0 to 63, all different within a row
Outputs:
- new_weight: float32 [64, 14336], P('fsdp')
- new_momentum: float32 [32, 64, 14336], P('rep', 'fsdp')
The draws below stay inside these ranges and needn't reach their ends.
Inputs may be any that keep to these rules, and one draw needn't show every extreme that they name: Each row of the window names 4 different bands, and every band is named by some row.
All inputs are finite; a program needn't handle non-finite values.
Results may differ from the reference program's by a relative error of at most 0.0003.
Values sent between devices are 32-bit elements; how exact they have to be, the bound alone decides.
A program may use at most 64 MiB of HBM per device.

```python
import jax
import jax.numpy as jnp
from jax import lax

TOK_DEV = 128
COLS = 14336
BAND = 64
KEEP = 4
RW = 64
SPANS = 224
TOKENS = 65536
N_REP = 32
N_FSDP = 16


def raised(values, stream_key, source, target, shards_of, factor):
    owner, partner = [(jnp.arange(values.shape[axis_at]) // (values.shape[axis_at] // shards_of)).reshape([-1 if axis == axis_at else 1 for axis in range(values.ndim)]) for axis_at in (source, target)]
    chosen = jax.random.permutation(stream_key, shards_of)[partner]
    strong = (owner == chosen) | (owner == (partner + shards_of // 2) % shards_of)
    return jnp.where(strong, factor * values, values)


def shard_levels(own_key, extent, pieces, least, top_value):
    loudness = 1.0
    for position, blocks in pieces:
        draws = jax.random.uniform(jax.random.fold_in(jax.random.fold_in(own_key, 6), position), (blocks,), jnp.float32, least / len(pieces), top_value / len(pieces))
        loudness = loudness * jnp.repeat(jnp.exp(draws), extent[position] // blocks).reshape((-1,) + (1,) * (len(extent) - 1 - position))
    return loudness


def distinct(own_key, rows, count, top, lift):
    ranking = jax.random.permutation(jax.random.fold_in(own_key, 1), count)
    boost = ranking
    for power in range(3):
        boost = boost * boost // count
    boost = boost * lift // count
    chance = jax.random.randint(jax.random.fold_in(own_key, 2), (rows, count), 0, 4096) + boost
    holders = jax.random.permutation(jax.random.fold_in(own_key, 3), rows)[jnp.arange(count) % rows]
    chance = jnp.where(jnp.arange(rows)[:, None] == holders[None, :], 1 << 14, chance)
    priority = chance * count + jnp.arange(count)
    return lax.top_k(priority.astype(jnp.int32), top)[1].astype(jnp.int32)


def scatter_about(rng, shape, spread, limit, split=(), kind=jnp.bfloat16):
    result = jax.random.normal(rng, shape, jnp.float32) * spread
    if len(split) > 0:
        result = shard_levels(rng, shape, split, -0.22, 0.18) * result
    return jnp.clip(result, min=-limit, max=limit).astype(kind)


def gaussian_with(own_key, extent, scale, reach, pieces, heavy, kind=jnp.bfloat16):
    result = scale * jax.random.normal(own_key, extent, jnp.float32)
    if pieces:
        result = result * shard_levels(own_key, extent, pieces, -0.22, 0.18)
    return jnp.clip(raised(result, jax.random.fold_in(own_key, 3), *heavy), -reach, reach).astype(kind)


def setup_inputs(seed: int = 0) -> dict:
    keys = jax.random.split(jax.random.key(seed), 6)
    return {
        "acts": gaussian_with(keys[0], (TOKENS, RW), 1.0, 16.0, ((0, 512),), (0, 1, 64, 4.0)),
        "cotangent": scatter_about(keys[1], (TOKENS, COLS), (TOK_DEV * N_FSDP) ** -0.5, 0.125, ((0, 512),)),
        "weight": scatter_about(keys[2], (RW, COLS), 8192 ** -0.5, 0.0625, ((0, 16),), jnp.float32),
        "momentum": scatter_about(keys[3], (N_REP, RW, COLS), 1.0, 6.0, ((0, 32), (1, 16)), jnp.float32),
        "bands": distinct(keys[4], RW, BAND, KEEP, 0),
    }


step_size = 2.0
decay = 0.999

def dct_table(width):
    index = jnp.arange(width, dtype=jnp.int32)
    freq = index.astype(jnp.float32)[:, None]
    place = index.astype(jnp.float32)[None, :]
    table = jnp.cos(jnp.pi * (2.0 * place + 1.0) * freq / (2.0 * width))
    scale = jnp.where(index == 0, jnp.sqrt(1.0 / width), jnp.sqrt(2.0 / width)).astype(jnp.float32)
    return table * scale[:, None]

def pick_rows(bands, width):
    onehot = (bands[:, :, None] == jnp.arange(width, dtype=jnp.int32)[None, None, :]).astype(jnp.float32)
    return jnp.einsum('rkm,mj->rkj', onehot, dct_table(width), precision=lax.Precision.HIGHEST)

def reference(acts, cotangent, weight, momentum, bands):
    group = N_FSDP * TOK_DEV
    inputs = acts.reshape(N_REP, group, RW)
    grads_out = cotangent.reshape(N_REP, group, COLS)
    picks = pick_rows(bands, BAND)

    def replica(item):
        local_in, local_out, state = item
        grad = jnp.dot(local_in.T, local_out, preferred_element_type=jnp.float32)
        moved = decay * state + grad
        blocks = moved.reshape(RW, SPANS, BAND)
        coefs = jnp.einsum('rcj,rkj->rkc', blocks, picks, precision=lax.Precision.HIGHEST)
        own = jnp.einsum('rkc,rkj->rcj', coefs, picks, precision=lax.Precision.HIGHEST)
        return (moved - own.reshape(RW, COLS), coefs)
    new_momentum, coefs = lax.map(replica, (inputs, grads_out, momentum))
    mean = lax.optimization_barrier(jnp.sum(coefs, axis=0)) / N_REP
    update = jnp.einsum('rkc,rkj->rcj', mean, picks, precision=lax.Precision.HIGHEST).reshape(RW, COLS)
    new_weight = weight - step_size * update
    return (new_weight, new_momentum)
```

```python
import jax
import jax.numpy as jnp
import numpy as np
from jax import lax
from jax.experimental import pallas as pl
from jax.experimental.pallas import tpu as pltpu
from jax.sharding import PartitionSpec as P

MESH = pl.DeviceIdType.MESH
F32, BF16 = jnp.float32, jnp.bfloat16

TOK, COLS, ROWS, BAND, KEEP = 128, 14336, 64, 64, 4
NZ, NY = 8, 8
OWN = 4
GROUP = 2048
GROUPS = COLS // GROUP
HALF = GROUP // 2
CHUNK = 512
TILES = GROUP // 128

STEP_SIZE = 2.0
DECAY = 0.999

UNITS = (
    [(3, 0), (3, 1), (4, 0), (4, 1), (-3, 0), (-3, 1)]
    + [(d, 1) for d in (-2, -1, 0, 1, 2)]
    + [(d, 0) for d in (-2, -1, 0, 1, 2)]
)
FAR_P, OPP, FAR_M = 0, 2, 4
CROSS = 6
HERE = 11


def table():
    band, place = np.arange(BAND)[None, :], np.arange(2 * BAND)[:, None] % BAND
    scale = np.where(band == 0, np.sqrt(1.0 / BAND), np.sqrt(2.0 / BAND))
    full = (scale * np.cos(np.pi * (2 * place + 1) * band / (2 * BAND))).astype(np.float32)
    high = full.astype(jnp.bfloat16)
    low = (full - high.astype(np.float32)).astype(jnp.bfloat16)
    return np.stack([high, low])


def cols_of(g, half=None):
    if half is None:
        return pl.ds(g * GROUP, GROUP)
    return pl.ds(g * GROUP + half * HALF, HALF)


def split(x):
    high = x.astype(BF16)
    return high, (x - high.astype(F32)).astype(BF16)


def by_row(x, row):
    return jnp.concatenate([jnp.where(row == i, x, 0.0) for i in range(OWN)], axis=1)


def kernel(
    bands, acts_hbm, cot_hbm, weight_hbm, momentum_hbm, table_hbm,
    new_weight, new_momentum,
    acts, cot, weight, momentum, tab, out_w, out_m,
    term, got4, got3p, got3m, gotx, got2p, got2m, got1p, got1m,
    wa_hi, wa_lo, wb_hi, wb_lo, quad, ring,
    load_sem, cot_sem, store_sem, send, recv, quad_send, quad_recv, ring_send, ring_recv,
):
    rep, fsdp = lax.axis_index("rep"), lax.axis_index("fsdp")
    z, me4 = rep // 4, lax.rem(rep, 4)
    xlo, core = me4 // 2, lax.rem(me4, 2)
    xhi, y = fsdp // NY, lax.rem(fsdp, NY)

    up = (rep, xhi * NY + lax.rem(y + 1, NY))
    down = (rep, xhi * NY + lax.rem(y + NY - 1, NY))
    across = (rep, (1 - xhi) * NY + y)
    quads = [
        (z * 4 + 2 * xlo + (1 - core), fsdp),
        (z * 4 + 2 * (1 - xlo) + core, fsdp),
        (z * 4 + 2 * (1 - xlo) + (1 - core), fsdp),
    ]
    rings = [(lax.rem(z + t, NZ) * 4 + me4, fsdp) for t in range(1, NZ)]

    loads = []
    for i, (src, dst) in enumerate(
        [(acts_hbm, acts), (table_hbm, tab), (momentum_hbm, momentum), (weight_hbm, weight)]
    ):
        loads.append(pltpu.make_async_copy(src, dst, load_sem.at[i]))
    cots = [
        pltpu.make_async_copy(cot_hbm.at[:, cols_of(g)], cot.at[:, cols_of(g)], cot_sem.at[g])
        for g in range(GROUPS)
    ]
    loads[0].start()
    cots[0].start()
    loads[1].start()
    for c in cots[1:]:
        c.start()
    loads[2].start()
    loads[3].start()

    barrier = pltpu.get_barrier_semaphore()
    friends = [up, down, across, *quads, *rings]
    for d in friends:
        pl.semaphore_signal(barrier, inc=1, device_id=d, device_id_type=MESH)

    sent = []
    counter = [0]

    def message(src, dst, device):
        n = counter[0]
        counter[0] += 1
        c = pltpu.make_async_remote_copy(
            src_ref=src, dst_ref=dst, send_sem=send.at[n], recv_sem=recv.at[n],
            device_id=device, device_id_type=MESH,
        )
        c.start()
        sent.append(c)
        return c

    loads[0].wait()
    place = lax.broadcasted_iota(jnp.int32, (ROWS, ROWS), 0)
    unit, sub = place // OWN, lax.rem(place, OWN)
    wanted = jnp.zeros((ROWS, ROWS), jnp.int32)
    for u, (d, r) in enumerate(UNITS):
        side = xhi if r == 0 else 1 - xhi
        owner = side * NY + lax.rem(y + d + NY, NY)
        wanted = jnp.where(unit == u, owner * OWN + sub, wanted)
    order = (wanted == lax.broadcasted_iota(jnp.int32, (ROWS, ROWS), 1)).astype(BF16)
    acts_t = lax.dot_general(
        order, acts[...], (((1,), (1,)), ((), ())), preferred_element_type=F32
    ).astype(BF16)

    m = {}

    def products(g):
        cots[g].wait()
        for s in range(GROUP // CHUNK):
            at = pl.ds(g * GROUP + s * CHUNK, CHUNK)
            out = jnp.dot(acts_t, cot[:, at], preferred_element_type=F32)
            for u in range(16):
                term[u, :, at] = out[u * OWN : (u + 1) * OWN]

    def first_sends(g):
        e, o = cols_of(g, 0), cols_of(g, 1)
        m["4p", g] = message(term.at[pl.ds(OPP, 2), :, e], got4.at[:, :, e], up)
        m["4m", g] = message(term.at[pl.ds(OPP, 2), :, o], got4.at[:, :, o], down)
        m["3p", g, 1] = message(term.at[pl.ds(FAR_P, 2), :, o], got3p.at[:, :, o], up)
        m["3m", g, 0] = message(term.at[pl.ds(FAR_M, 2), :, e], got3m.at[:, :, e], down)

    def x_one(g):
        c = cols_of(g)
        m["x1p", g] = message(term.at[CROSS + 3, :, c], gotx.at[3, :, c], across)
        m["x1m", g] = message(term.at[CROSS + 1, :, c], gotx.at[1, :, c], across)

    def x_zero(g):
        c = cols_of(g)
        m["x0", g] = message(term.at[CROSS + 2, :, c], gotx.at[2, :, c], across)

    def step_b(g):
        e, o = cols_of(g, 0), cols_of(g, 1)
        m["4p", g].wait_recv()
        term[FAR_P : FAR_P + 2, :, e] += got4[:, :, e]
        m["3p", g, 0] = message(term.at[pl.ds(FAR_P, 2), :, e], got3p.at[:, :, e], up)
        m["4m", g].wait_recv()
        term[FAR_M : FAR_M + 2, :, o] += got4[:, :, o]
        m["3m", g, 1] = message(term.at[pl.ds(FAR_M, 2), :, o], got3m.at[:, :, o], down)

    def step_c(g, free):
        hp, hm = (1, 0) if free else (0, 1)
        c = cols_of(g, hp)
        m["3p", g, hp].wait_recv()
        term[CROSS + 4, :, c] += got3p[1, :, c]
        m["x2p", g, hp] = message(term.at[CROSS + 4, :, c], gotx.at[4, :, c], across)
        term[HERE + 4, :, c] += got3p[0, :, c]
        c = cols_of(g, hm)
        m["3m", g, hm].wait_recv()
        term[CROSS, :, c] += got3m[1, :, c]
        m["x2m", g, hm] = message(term.at[CROSS, :, c], gotx.at[0, :, c], across)
        term[HERE, :, c] += got3m[0, :, c]

    def step_d(g):
        c = cols_of(g)
        m["x2p", g, 0].wait_recv()
        m["x2p", g, 1].wait_recv()
        term[HERE + 4, :, c] += gotx[4, :, c]
        m["2p", g] = message(term.at[HERE + 4, :, c], got2p.at[:, c], up)
        m["x2m", g, 0].wait_recv()
        m["x2m", g, 1].wait_recv()
        term[HERE, :, c] += gotx[0, :, c]
        m["2m", g] = message(term.at[HERE, :, c], got2m.at[:, c], down)

    def step_e(g):
        c = cols_of(g)
        m["x1p", g].wait_recv()
        m["2p", g].wait_recv()
        term[HERE + 3, :, c] += got2p[:, c] + gotx[3, :, c]
        m["1p", g] = message(term.at[HERE + 3, :, c], got1p.at[:, c], up)
        m["x1m", g].wait_recv()
        m["2m", g].wait_recv()
        term[HERE + 1, :, c] += got2m[:, c] + gotx[1, :, c]
        m["1m", g] = message(term.at[HERE + 1, :, c], got1m.at[:, c], down)

    row = lax.rem(lax.broadcasted_iota(jnp.int32, (OWN * TILES, 128), 0), OWN)
    tile = lax.broadcasted_iota(jnp.int32, (OWN * TILES, 128), 0) // OWN
    lane8 = lax.broadcasted_iota(jnp.int32, (OWN * TILES, 128), 1) // (2 * KEEP)
    mine = tile == lane8

    def picks():
        loads[1].wait()
        lane = lax.broadcasted_iota(jnp.int32, (BAND, 128), 1)
        band = lax.broadcasted_iota(jnp.int32, (BAND, 128), 0)
        c = lax.broadcasted_iota(jnp.int32, (128, 128), 0)
        l = lax.broadcasted_iota(jnp.int32, (128, 128), 1)
        same = c // BAND == lax.rem(l // KEEP, 2)
        for i in range(OWN):
            want = jnp.zeros((BAND, 128), jnp.int32)
            for k in range(KEEP):
                want = jnp.where(lax.rem(lane, KEEP) == k, bands[i, k], want)
            onehot = (want == band).astype(BF16)
            for t, wa, wb in ((0, wa_hi, wb_hi), (1, wa_lo, wb_lo)):
                w = jnp.dot(tab[t], onehot, preferred_element_type=F32)
                w = jnp.where(same, w, 0.0).astype(BF16)
                wa[i * 128 : (i + 1) * 128, :] = w
                wb[:, i * 128 : (i + 1) * 128] = w

    def spread(coefs):
        hi, lo = split(by_row(coefs, row))
        nt = (((1,), (1,)), ((), ()))
        out = lax.dot_general(hi, wb_hi[...], nt, preferred_element_type=F32)
        out += lax.dot_general(hi, wb_lo[...], nt, preferred_element_type=F32)
        out += lax.dot_general(lo, wb_hi[...], nt, preferred_element_type=F32)
        return jnp.concatenate([out[j * OWN : (j + 1) * OWN] for j in range(TILES)], axis=1)

    stores = []

    def step_f(g):
        c = cols_of(g)
        m["x0", g].wait_recv()
        m["1p", g].wait_recv()
        m["1m", g].wait_recv()
        grad = (term[HERE + 2, :, c] + gotx[2, :, c]) + (got1p[:, c] + got1m[:, c])
        moved = DECAY * momentum[0, :, c] + grad
        x = jnp.concatenate([moved[:, j * 128 : (j + 1) * 128] for j in range(TILES)], axis=0)
        hi, lo = split(by_row(x, row))
        coefs = jnp.dot(hi, wa_hi[...], preferred_element_type=F32)
        coefs += jnp.dot(hi, wa_lo[...], preferred_element_type=F32)
        coefs += jnp.dot(lo, wa_hi[...], preferred_element_type=F32)
        coefs = jnp.where(mine, coefs, 0.0)
        dense = coefs[0:OWN]
        for j in range(1, TILES):
            dense += coefs[j * OWN : (j + 1) * OWN]
        quad[me4, g] = dense
        return c, moved, coefs

    def finish_momentum(g, c, moved, coefs):
        out_m[0, :, c] = moved - spread(coefs)
        s = pltpu.make_async_copy(out_m.at[:, :, c], new_momentum.at[:, :, c], store_sem.at[0, g])
        s.start()
        stores.append(s)

    BATCHES = [(0, 3), (3, 6), (6, 7)]
    q, v = {}, {}

    def quad_sends(b):
        g0, g1 = BATCHES[b]
        q[b] = []
        for t, d in enumerate(quads):
            part = quad.at[me4, pl.ds(g0, g1 - g0)]
            c = pltpu.make_async_remote_copy(
                src_ref=part, dst_ref=part, send_sem=quad_send.at[b, t], recv_sem=quad_recv.at[b, t],
                device_id=d, device_id_type=MESH,
            )
            c.start()
            q[b].append(c)

    def ring_sends(b):
        g0, g1 = BATCHES[b]
        for c in q[b]:
            c.wait_recv()
        s = slice(g0, g1)
        ring[z, s] = (quad[0, s] + quad[1, s]) + (quad[2, s] + quad[3, s])
        v[b] = []
        part = ring.at[z, pl.ds(g0, g1 - g0)]
        for t, d in enumerate(rings):
            c = pltpu.make_async_remote_copy(
                src_ref=part, dst_ref=part, send_sem=ring_send.at[b, t], recv_sem=ring_recv.at[b, t],
                device_id=d, device_id_type=MESH,
            )
            c.start()
            v[b].append(c)

    def weights(b):
        g0, g1 = BATCHES[b]
        for c in v[b]:
            c.wait_recv()
        for g in range(g0, g1):
            total = ring[0, g]
            for k in range(1, NZ):
                total += ring[k, g]
            mean = total * (1.0 / 32)
            rows = jnp.concatenate([mean] * TILES, axis=0)
            c = cols_of(g)
            out_w[:, c] = weight[:, c] - STEP_SIZE * spread(jnp.where(mine, rows, 0.0))
            s = pltpu.make_async_copy(out_w.at[:, c], new_weight.at[:, c], store_sem.at[1, g])
            s.start()
            stores.append(s)

    products(0)
    pl.semaphore_wait(barrier, len(friends))
    first_sends(0)
    x_one(0)
    for g in range(1, GROUPS):
        products(g)
        first_sends(g)
        if g < 4:
            x_one(g)
    for g in range(GROUPS):
        step_b(g)
        step_c(g, True)
        if g in (2, 4):
            x_one(4 if g == 2 else 5)
    picks()
    loads[2].wait()
    loads[3].wait()
    events = (
        [(17.4 + g, "c", g) for g in range(GROUPS)]
        + [(22.2 + g, "d", g) for g in range(GROUPS)]
        + [(25.5 + g, "e", g) for g in range(GROUPS)]
        + [(32.5 + g, "f", g) for g in range(GROUPS)]
        + [(23.45, "x1", 6)]
        + [(23.5 + 0.9 * g, "x0", g) for g in range(GROUPS)]
    )
    late = []
    for _, kind, g in sorted(events):
        if kind == "c":
            step_c(g, False)
        elif kind == "d":
            step_d(g)
        elif kind == "e":
            step_e(g)
        elif kind == "x1":
            x_one(g)
        elif kind == "x0":
            x_zero(g)
        else:
            held = step_f(g)
            for b, (g0, g1) in enumerate(BATCHES):
                if g == g1 - 1:
                    quad_sends(b)
            finish_momentum(g, *held)
            if g == 4:
                ring_sends(0)
    ring_sends(1)
    weights(0)
    ring_sends(2)
    weights(1)
    for c in sent:
        c.wait_send()
    for cs in (*q.values(), *v.values()):
        for c in cs:
            c.wait_send()
    weights(2)
    for s in stores:
        s.wait()


MESSAGES = 18 * GROUPS


def on_device(acts, cotangent, weight, momentum, bands):
    any_space = pl.BlockSpec(memory_space=pl.ANY)
    unit = lambda *lead: pltpu.VMEM((*lead, OWN, COLS), F32)
    dma = lambda *shape: pltpu.SemaphoreType.DMA(shape)
    return pl.pallas_call(
        kernel,
        out_shape=(
            jax.ShapeDtypeStruct((OWN, COLS), F32),
            jax.ShapeDtypeStruct((1, OWN, COLS), F32),
        ),
        in_specs=[pl.BlockSpec(memory_space=pltpu.SMEM)] + [any_space] * 5,
        out_specs=(any_space, any_space),
        scratch_shapes=[
            pltpu.VMEM((TOK, ROWS), BF16),
            pltpu.VMEM((TOK, COLS), BF16),
            unit(), unit(1),
            pltpu.VMEM((2, 2 * BAND, BAND), BF16),
            unit(), unit(1),
            unit(16), unit(2), unit(2), unit(2), unit(5), unit(), unit(), unit(), unit(),
            pltpu.VMEM((OWN * 128, 128), BF16), pltpu.VMEM((OWN * 128, 128), BF16),
            pltpu.VMEM((128, OWN * 128), BF16), pltpu.VMEM((128, OWN * 128), BF16),
            pltpu.VMEM((4, GROUPS, OWN, 128), F32), pltpu.VMEM((NZ, GROUPS, OWN, 128), F32),
            dma(4), dma(GROUPS), dma(2, GROUPS), dma(MESSAGES), dma(MESSAGES),
            dma(3, 3), dma(3, 3), dma(3, 7), dma(3, 7),
        ],
        compiler_params=pltpu.CompilerParams(
            collective_id=0, has_side_effects=True, vmem_limit_bytes=48 * 2**20
        ),
    )(bands, acts, cotangent, weight, momentum, jnp.asarray(table()))


def solution(mesh):
    placed = (
        P(("rep", "fsdp"), None),
        P(("rep", "fsdp"), None),
        P("fsdp", None),
        P("rep", "fsdp", None),
        P("fsdp", None),
    )
    return jax.shard_map(
        on_device,
        mesh=mesh,
        in_specs=placed,
        out_specs=(P("fsdp", None), P("rep", "fsdp", None)),
        check_vma=False,
    )
```

```python
import jax
import jax.numpy as jnp
import numpy as np
from jax import lax
from jax.experimental import pallas as pl
from jax.experimental.pallas import tpu as pltpu
from jax.sharding import PartitionSpec as P

MESH = pl.DeviceIdType.MESH
F32, BF16 = jnp.float32, jnp.bfloat16

TOK, COLS, ROWS, BAND, KEEP = 128, 14336, 64, 64, 4
NZ, NY = 8, 8
OWN = 4
OWNERS = ROWS // OWN
GROUP = 2048
GROUPS = COLS // GROUP
HALF = GROUP // 2
CHUNK = 512
TILES = GROUP // 128
BATCHES = [(0, 3), (3, 6), (6, 7)]

STEP_SIZE = 2.0
DECAY = 0.999


def table():
    band, place = np.arange(BAND)[None, :], np.arange(2 * BAND)[:, None] % BAND
    scale = np.where(band == 0, np.sqrt(1.0 / BAND), np.sqrt(2.0 / BAND))
    full = (scale * np.cos(np.pi * (2 * place + 1) * band / (2 * BAND))).astype(np.float32)
    high = full.astype(jnp.bfloat16)
    low = (full - high.astype(np.float32)).astype(jnp.bfloat16)
    return np.stack([high, low])


def cols_of(g, half=None):
    if half is None:
        return pl.ds(g * GROUP, GROUP)
    return pl.ds(g * GROUP + half * HALF, HALF)


def split(x):
    high = x.astype(BF16)
    return high, (x - high.astype(F32)).astype(BF16)


def iota(shape, axis):
    return lax.broadcasted_iota(jnp.int32, shape, axis)


def by_row(x):
    row = lax.rem(iota(x.shape, 0), OWN)
    return jnp.concatenate([jnp.where(row == i, x, 0.0) for i in range(OWN)], axis=1)


def own_lanes(x):
    tile = lax.rem(iota(x.shape, 0) // OWN, TILES)
    return jnp.where(tile == iota(x.shape, 1) // (2 * KEEP), x, 0.0)


def stacked(x):
    return jnp.concatenate([x[:, j * 128 : (j + 1) * 128] for j in range(x.shape[1] // 128)], axis=0)


def unstacked(x):
    return jnp.concatenate([x[j * OWN : (j + 1) * OWN] for j in range(x.shape[0] // OWN)], axis=1)


def kernel(
    bands_hbm, acts_hbm, cot_hbm, weight_hbm, momentum_hbm, table_hbm,
    new_weight, new_momentum,
    bands, acts, cot, weight, momentum, tab,
    term, got4, got3p, got3m, gotx, got2p, got2m, got1p, got1m,
    wa_hi, wa_lo, wb_hi, wb_lo, quad, ring,
    load_sem, cot_sem, recv, send, rep_recv, rep_send,
):
    rep, fsdp = lax.axis_index("rep"), lax.axis_index("fsdp")
    z, me4 = rep // 4, lax.rem(rep, 4)
    xlo, core = me4 // 2, lax.rem(me4, 2)
    xhi, y = fsdp // NY, lax.rem(fsdp, NY)

    up = (rep, xhi * NY + lax.rem(y + 1, NY))
    down = (rep, xhi * NY + lax.rem(y + NY - 1, NY))
    across = (rep, (1 - xhi) * NY + y)
    quads = [
        (z * 4 + 2 * xlo + (1 - core), fsdp),
        (z * 4 + 2 * (1 - xlo) + core, fsdp),
        (z * 4 + 2 * (1 - xlo) + (1 - core), fsdp),
    ]
    rings = [(lax.rem(z + t, NZ) * 4 + me4, fsdp) for t in (4, 3, 5, 2, 6, 1, 7)]

    loads = [
        pltpu.make_async_copy(src, dst, load_sem.at[i])
        for i, (src, dst) in enumerate(
            [(acts_hbm, acts), (table_hbm, tab), (momentum_hbm, momentum), (weight_hbm, weight), (bands_hbm, bands)]
        )
    ]
    cots = [
        pltpu.make_async_copy(cot_hbm.at[:, cols_of(g)], cot.at[:, cols_of(g)], cot_sem.at[g])
        for g in range(GROUPS)
    ]
    loads[0].start()
    for c in cots:
        c.start()
    for c in loads[1:]:
        c.start()

    barrier = pltpu.get_barrier_semaphore()
    friends = [up, down, across, *quads, *rings]
    for d in friends:
        pl.semaphore_signal(barrier, inc=1, device_id=d, device_id_type=MESH)

    def message(src, dst, device, kind, g):
        pltpu.make_async_remote_copy(
            src_ref=src, dst_ref=dst, send_sem=send.at[0], recv_sem=recv.at[kind, g],
            device_id=device, device_id_type=MESH,
        ).start()

    def landed(ref, sem):
        pltpu.make_async_copy(ref, ref, sem).wait()

    K4, K3F, K3D, KX, KE, KF = range(6)

    def products(g):
        cots[g].wait()
        for s in range(GROUP // CHUNK):
            at = pl.ds(g * GROUP + s * CHUNK, CHUNK)
            out = jnp.dot(acts[...], cot[:, at], preferred_element_type=F32)
            for o in range(OWNERS):
                r = xhi if o < NY else 1 - xhi
                u = 2 * lax.rem(o % NY - y + NY, NY) + r
                term[u, :, at] = out[o * OWN : (o + 1) * OWN]

    def first_sends(g):
        e, o = cols_of(g, 0), cols_of(g, 1)
        message(term.at[pl.ds(8, 2), :, e], got4.at[:, :, e], up, K4, g)
        message(term.at[pl.ds(8, 2), :, o], got4.at[:, :, o], down, K4, g)
        message(term.at[pl.ds(6, 2), :, o], got3p.at[:, :, o], up, K3F, g)
        message(term.at[pl.ds(10, 2), :, e], got3m.at[:, :, e], down, K3F, g)

    def x_one(g):
        c = cols_of(g)
        message(term.at[3, :, c], gotx.at[1, :, c], across, KE, g)
        message(term.at[15, :, c], gotx.at[4, :, c], across, KE, g)

    def x_zero(g):
        c = cols_of(g)
        message(term.at[1, :, c], gotx.at[0, :, c], across, KF, g)

    def step_b(g):
        e, o = cols_of(g, 0), cols_of(g, 1)
        landed(got4.at[:, :, cols_of(g)], recv.at[K4, g])
        term[6:8, :, e] += got4[:, :, e]
        message(term.at[pl.ds(6, 2), :, e], got3p.at[:, :, e], up, K3D, g)
        term[10:12, :, o] += got4[:, :, o]
        message(term.at[pl.ds(10, 2), :, o], got3m.at[:, :, o], down, K3D, g)

    def step_c(g, kind):
        landed(got3p.at[:, :, cols_of(g)], recv.at[kind, g])
        c = cols_of(g, 1 if kind == K3F else 0)
        term[5, :, c] += got3p[1, :, c]
        message(term.at[5, :, c], gotx.at[2, :, c], across, KX, g)
        term[4, :, c] += got3p[0, :, c]
        c = cols_of(g, 0 if kind == K3F else 1)
        term[13, :, c] += got3m[1, :, c]
        message(term.at[13, :, c], gotx.at[3, :, c], across, KX, g)
        term[12, :, c] += got3m[0, :, c]

    def step_d(g):
        c = cols_of(g)
        landed(gotx.at[pl.ds(2, 2), :, c], recv.at[KX, g])
        term[4, :, c] += gotx[2, :, c]
        message(term.at[4, :, c], got2p.at[:, c], up, KE, g)
        term[12, :, c] += gotx[3, :, c]
        message(term.at[12, :, c], got2m.at[:, c], down, KE, g)

    def step_e(g):
        c = cols_of(g)
        landed(gotx.at[pl.ds(1, 4), :, c], recv.at[KE, g])
        term[2, :, c] += got2p[:, c] + gotx[1, :, c]
        message(term.at[2, :, c], got1p.at[:, c], up, KF, g)
        term[14, :, c] += got2m[:, c] + gotx[4, :, c]
        message(term.at[14, :, c], got1m.at[:, c], down, KF, g)

    def picks():
        for c in loads[1:]:
            c.wait()
        lane, band = iota((BAND, 128), 1), iota((BAND, 128), 0)
        same = iota((128, 128), 0) // BAND == lax.rem(iota((128, 128), 1) // KEEP, 2)
        for i in range(OWN):
            want = jnp.zeros((BAND, 128), jnp.int32)
            for k in range(KEEP):
                want = jnp.where(lax.rem(lane, KEEP) == k, bands[i, k], want)
            onehot = (want == band).astype(BF16)
            for t, wa, wb in ((0, wa_hi, wb_hi), (1, wa_lo, wb_lo)):
                w = jnp.dot(tab[t], onehot, preferred_element_type=F32)
                w = jnp.where(same, w, 0.0).astype(BF16)
                wa[i * 128 : (i + 1) * 128, :] = w
                wb[:, i * 128 : (i + 1) * 128] = w

    def spread(coefs):
        hi, lo = split(by_row(coefs))
        nt = (((1,), (1,)), ((), ()))
        out = lax.dot_general(hi, wb_hi[...], nt, preferred_element_type=F32)
        out += lax.dot_general(hi, wb_lo[...], nt, preferred_element_type=F32)
        out += lax.dot_general(lo, wb_hi[...], nt, preferred_element_type=F32)
        return unstacked(out)

    held = {}

    def step_f(g):
        c = cols_of(g)
        landed(gotx.at[pl.ds(0, 3), :, c], recv.at[KF, g])
        grad = (term[0, :, c] + gotx[0, :, c]) + (got1p[:, c] + got1m[:, c])
        moved = DECAY * momentum[0, :, c] + grad
        hi, lo = split(by_row(stacked(moved)))
        coefs = jnp.dot(hi, wa_hi[...], preferred_element_type=F32)
        coefs += jnp.dot(hi, wa_lo[...], preferred_element_type=F32)
        coefs += jnp.dot(lo, wa_hi[...], preferred_element_type=F32)
        coefs = own_lanes(coefs)
        dense = coefs[0:OWN]
        for j in range(1, TILES):
            dense += coefs[j * OWN : (j + 1) * OWN]
        quad[me4, g] = dense
        held[g] = moved, coefs

    def finish_momentum(g):
        moved, coefs = held.pop(g)
        new_momentum[0, :, cols_of(g)] = moved - spread(coefs)

    def rep_message(ref, device, kind, b):
        pltpu.make_async_remote_copy(
            src_ref=ref, dst_ref=ref, send_sem=rep_send.at[kind], recv_sem=rep_recv.at[kind, b],
            device_id=device, device_id_type=MESH,
        ).start()

    def quad_sends(b):
        g0, g1 = BATCHES[b]
        for d in quads:
            rep_message(quad.at[me4, pl.ds(g0, g1 - g0)], d, 0, b)

    def ring_sends(b):
        g0, g1 = BATCHES[b]
        landed(quad.at[pl.ds(0, 3), pl.ds(g0, g1 - g0)], rep_recv.at[0, b])
        s = slice(g0, g1)
        ring[z, s] = (quad[0, s] + quad[1, s]) + (quad[2, s] + quad[3, s])
        for d in rings:
            rep_message(ring.at[z, pl.ds(g0, g1 - g0)], d, 1, b)

    def weights(b):
        g0, g1 = BATCHES[b]
        landed(ring.at[pl.ds(0, NZ - 1), pl.ds(g0, g1 - g0)], rep_recv.at[1, b])
        rows = []
        for g in range(g0, g1):
            total = ring[0, g]
            for k in range(1, NZ):
                total += ring[k, g]
            rows += [total * (1.0 / 32)] * TILES
        update = spread(own_lanes(jnp.concatenate(rows, axis=0)))
        c = pl.ds(g0 * GROUP, (g1 - g0) * GROUP)
        new_weight[:, c] = weight[:, c] - STEP_SIZE * update

    loads[0].wait()
    products(0)
    pl.semaphore_wait(barrier, len(friends))
    first_sends(0)
    x_one(0)
    for g in range(1, GROUPS):
        products(g)
        first_sends(g)
        if g < 4:
            x_one(g)
    for g in range(GROUPS):
        step_b(g)
        step_c(g, K3F)
        if g in (2, 4):
            x_one(4 if g == 2 else 5)
    picks()
    events = (
        [(17.4 + g, step_c, g, K3D) for g in range(GROUPS)]
        + [(22.2 + g, step_d, g) for g in range(GROUPS)]
        + [(25.5 + g, step_e, g) for g in range(GROUPS)]
        + [(32.5 + g, step_f, g) for g in range(GROUPS)]
        + [(32.55 + g1 - 1, quad_sends, b) for b, (_, g1) in enumerate(BATCHES)]
        + [(32.6 + g, finish_momentum, g) for g in range(GROUPS)]
        + [(23.45, x_one, 6)]
        + [(23.5 + 0.9 * g, x_zero, g) for g in range(GROUPS)]
        + [(38.57, ring_sends, 0), (38.8, ring_sends, 1), (38.9, ring_sends, 2)]
        + [(39 + b, weights, b) for b in range(len(BATCHES))]
    )
    for _, f, *args in sorted(events, key=lambda e: e[0]):
        f(*args)
    landed(term.at[pl.ds(0, 15)], send.at[0])
    landed(quad.at[pl.ds(0, 3)], rep_send.at[0])
    landed(ring.at[pl.ds(0, 7)], rep_send.at[1])


def hand_out(weight, momentum, new_weight, new_momentum, sem):
    copies = [
        pltpu.make_async_copy(weight, new_weight, sem.at[0]),
        pltpu.make_async_copy(momentum, new_momentum, sem.at[1]),
    ]
    for c in copies:
        c.start()
    for c in copies:
        c.wait()


def on_device(acts, cotangent, weight, momentum, bands):
    hbm = pl.BlockSpec(memory_space=pltpu.HBM)
    vmem = pl.BlockSpec(memory_space=pltpu.VMEM)
    unit = lambda *lead: pltpu.VMEM((*lead, OWN, COLS), F32)
    dma = lambda *shape: pltpu.SemaphoreType.DMA(shape)
    results = pl.pallas_call(
        kernel,
        out_shape=(pltpu.VMEM((OWN, COLS), F32), pltpu.VMEM((1, OWN, COLS), F32)),
        in_specs=[hbm] * 6,
        out_specs=(vmem, vmem),
        scratch_shapes=[
            pltpu.SMEM((OWN, KEEP), jnp.int32),
            pltpu.VMEM((ROWS, TOK), BF16),
            pltpu.VMEM((TOK, COLS), BF16),
            unit(), unit(1),
            pltpu.VMEM((2, 2 * BAND, BAND), BF16),
            unit(16), unit(2), unit(2), unit(2), unit(5), unit(), unit(), unit(), unit(),
            pltpu.VMEM((OWN * 128, 128), BF16), pltpu.VMEM((OWN * 128, 128), BF16),
            pltpu.VMEM((128, OWN * 128), BF16), pltpu.VMEM((128, OWN * 128), BF16),
            pltpu.VMEM((4, GROUPS, OWN, 128), F32), pltpu.VMEM((NZ, GROUPS, OWN, 128), F32),
            dma(5), dma(GROUPS), dma(6, GROUPS), dma(1), dma(2, len(BATCHES)), dma(2),
        ],
        compiler_params=pltpu.CompilerParams(
            collective_id=0, has_side_effects=True, vmem_limit_bytes=40 * 2**20
        ),
    )(*(pltpu.with_memory_space_constraint(a, pltpu.HBM) for a in (bands, acts.T, cotangent, weight, momentum, jnp.asarray(table()))))
    return pl.pallas_call(
        hand_out,
        out_shape=(
            jax.ShapeDtypeStruct((OWN, COLS), F32),
            jax.ShapeDtypeStruct((1, OWN, COLS), F32),
        ),
        in_specs=[pl.BlockSpec(memory_space=pl.ANY)] * 2,
        out_specs=(hbm, hbm),
        scratch_shapes=[dma(2)],
        compiler_params=pltpu.CompilerParams(vmem_limit_bytes=2**20),
    )(*(pltpu.with_memory_space_constraint(a, pltpu.VMEM) for a in results))


def solution(mesh):
    placed = (
        P(("rep", "fsdp"), None),
        P(("rep", "fsdp"), None),
        P("fsdp", None),
        P("rep", "fsdp", None),
        P("fsdp", None),
    )
    return jax.shard_map(
        on_device,
        mesh=mesh,
        in_specs=placed,
        out_specs=(P("fsdp", None), P("rep", "fsdp", None)),
        check_vma=False,
    )
```

```python
import jax
import jax.numpy as jnp
import numpy as np
from jax import lax
from jax.experimental import pallas as pl
from jax.experimental.pallas import tpu as pltpu
from jax.sharding import PartitionSpec as P

MESH = pl.DeviceIdType.MESH
F32, BF16 = jnp.float32, jnp.bfloat16

TOK, COLS, ROWS, BAND, KEEP = 128, 14336, 64, 64, 4
NY = 8
CHIPS = 16
FARTHEST_FIRST = (8, 9, 7, 6, 10, 5, 11, 4, 12, 3, 13, 2, 14, 1, 15)
OWN = 4
OWNERS = ROWS // OWN
GROUP = 2048
GROUPS = COLS // GROUP
HALF = GROUP // 2
CHUNK = 512
TILES = GROUP // 128
BATCHES = [(0, 3), (3, 6), (6, 7)]

STEP_SIZE = 2.0
DECAY = 0.999


def table():
    band, place = np.arange(BAND)[None, :], np.arange(2 * BAND)[:, None] % BAND
    scale = np.where(band == 0, np.sqrt(1.0 / BAND), np.sqrt(2.0 / BAND))
    full = (scale * np.cos(np.pi * (2 * place + 1) * band / (2 * BAND))).astype(np.float32)
    high = full.astype(jnp.bfloat16)
    low = (full - high.astype(np.float32)).astype(jnp.bfloat16)
    return np.stack([high, low])


def cols_of(g, half=None):
    if half is None:
        return pl.ds(g * GROUP, GROUP)
    return pl.ds(g * GROUP + half * HALF, HALF)


def split(x):
    high = x.astype(BF16)
    return high, (x - high.astype(F32)).astype(BF16)


def iota(shape, axis):
    return lax.broadcasted_iota(jnp.int32, shape, axis)


def by_row(x):
    row = lax.rem(iota(x.shape, 0), OWN)
    return jnp.concatenate([jnp.where(row == i, x, 0.0) for i in range(OWN)], axis=1)


def own_lanes(x):
    tile = lax.rem(iota(x.shape, 0) // OWN, TILES)
    return jnp.where(tile == iota(x.shape, 1) // (2 * KEEP), x, 0.0)


def stacked(x):
    return jnp.concatenate([x[:, j * 128 : (j + 1) * 128] for j in range(x.shape[1] // 128)], axis=0)


def unstacked(x):
    return jnp.concatenate([x[j * OWN : (j + 1) * OWN] for j in range(x.shape[0] // OWN)], axis=1)


def kernel(
    bands_hbm, acts_hbm, cot_hbm, weight_hbm, momentum_hbm, table_hbm,
    new_weight, new_momentum,
    bands, acts, cot, weight, momentum, tab,
    term, got4, got3p, got3m, gotx, got2p, got2m, got1p, got1m,
    wa_hi, wa_lo, wb_hi, wb_lo, pair, ring,
    load_sem, cot_sem, recv, send, rep_recv, rep_send, there,
):
    rep, fsdp = lax.axis_index("rep"), lax.axis_index("fsdp")
    chip, core = rep // 2, lax.rem(rep, 2)
    xhi, y = fsdp // NY, lax.rem(fsdp, NY)

    up = (rep, xhi * NY + lax.rem(y + 1, NY))
    down = (rep, xhi * NY + lax.rem(y + NY - 1, NY))
    across = (rep, (1 - xhi) * NY + y)
    beside = (2 * chip + (1 - core), fsdp)
    others = [(2 * lax.rem(chip + t, CHIPS) + core, fsdp) for t in FARTHEST_FIRST]

    loads = [
        pltpu.make_async_copy(src, dst, load_sem.at[i])
        for i, (src, dst) in enumerate(
            [(acts_hbm, acts), (table_hbm, tab), (momentum_hbm, momentum), (weight_hbm, weight), (bands_hbm, bands)]
        )
    ]
    cots = [
        pltpu.make_async_copy(cot_hbm.at[:, cols_of(g)], cot.at[:, cols_of(g)], cot_sem.at[g])
        for g in range(GROUPS)
    ]
    loads[0].start()
    for c in cots:
        c.start()
    for c in loads[1:]:
        c.start()

    barrier = pltpu.get_barrier_semaphore()
    for d in (up, down, across):
        pl.semaphore_signal(barrier, inc=1, device_id=d, device_id_type=MESH)

    def tell(sem, first, last):
        @pl.loop(first, last)
        def _(i):
            pl.semaphore_signal(sem, inc=1, device_id=(2 * i + core, fsdp), device_id_type=MESH)

    tell(barrier, chip + 1, CHIPS)

    @pl.when(core == 0)
    def _():
        pl.semaphore_signal(barrier, inc=1, device_id=beside, device_id_type=MESH)

    def enter():
        pl.semaphore_wait(barrier, 3 + chip + core)

    def answer():
        tell(there.at[0], 0, chip)

        @pl.when(core == 1)
        def _():
            pl.semaphore_signal(there.at[1], inc=1, device_id=beside, device_id_type=MESH)

    def all_there():
        @pl.when(core == 0)
        def _():
            pl.semaphore_wait(there.at[1], 1)

        @pl.when(chip < CHIPS - 1)
        def _():
            pl.semaphore_wait(there.at[0], CHIPS - 1 - chip)

    def message(src, dst, device, kind, g):
        pltpu.make_async_remote_copy(
            src_ref=src, dst_ref=dst, send_sem=send.at[0], recv_sem=recv.at[kind, g],
            device_id=device, device_id_type=MESH,
        ).start()

    def landed(ref, sem):
        pltpu.make_async_copy(ref, ref, sem).wait()

    K4, K3F, K3D, KXF, KXD, KE, KF = range(7)

    def products(g):
        cots[g].wait()
        for s in range(GROUP // CHUNK):
            at = pl.ds(g * GROUP + s * CHUNK, CHUNK)
            out = jnp.dot(acts[...], cot[:, at], preferred_element_type=F32)
            for o in range(OWNERS):
                r = xhi if o < NY else 1 - xhi
                u = 2 * lax.rem(o % NY - y + NY, NY) + r
                term[u, :, at] = out[o * OWN : (o + 1) * OWN]

    def first_sends(g):
        e, o = cols_of(g, 0), cols_of(g, 1)
        message(term.at[pl.ds(8, 2), :, e], got4.at[:, :, e], up, K4, g)
        message(term.at[pl.ds(8, 2), :, o], got4.at[:, :, o], down, K4, g)
        message(term.at[pl.ds(6, 2), :, o], got3p.at[:, :, o], up, K3F, g)
        message(term.at[pl.ds(10, 2), :, e], got3m.at[:, :, e], down, K3F, g)

    def x_one(g):
        c = cols_of(g)
        message(term.at[3, :, c], gotx.at[1, :, c], across, KE, g)
        message(term.at[15, :, c], gotx.at[4, :, c], across, KE, g)

    def x_zero(g):
        c = cols_of(g)
        message(term.at[1, :, c], gotx.at[0, :, c], across, KF, g)

    def step_b(g):
        e, o = cols_of(g, 0), cols_of(g, 1)
        landed(got4.at[:, :, cols_of(g)], recv.at[K4, g])
        term[6:8, :, e] += got4[:, :, e]
        message(term.at[pl.ds(6, 2), :, e], got3p.at[:, :, e], up, K3D, g)
        term[10:12, :, o] += got4[:, :, o]
        message(term.at[pl.ds(10, 2), :, o], got3m.at[:, :, o], down, K3D, g)

    def step_c(g, kind):
        landed(got3p.at[:, :, cols_of(g)], recv.at[kind, g])
        then = KXF if kind == K3F else KXD
        c = cols_of(g, 1 if kind == K3F else 0)
        term[5, :, c] += got3p[1, :, c]
        message(term.at[5, :, c], gotx.at[2, :, c], across, then, g)
        term[4, :, c] += got3p[0, :, c]
        c = cols_of(g, 0 if kind == K3F else 1)
        term[13, :, c] += got3m[1, :, c]
        message(term.at[13, :, c], gotx.at[3, :, c], across, then, g)
        term[12, :, c] += got3m[0, :, c]

    def step_d(g, kind):
        landed(gotx.at[pl.ds(2, 2), :, cols_of(g, 0)], recv.at[kind, g])
        c = cols_of(g, 1 if kind == KXF else 0)
        term[4, :, c] += gotx[2, :, c]
        message(term.at[4, :, c], got2p.at[:, c], up, KE, g)
        c = cols_of(g, 0 if kind == KXF else 1)
        term[12, :, c] += gotx[3, :, c]
        message(term.at[12, :, c], got2m.at[:, c], down, KE, g)

    def step_e(g):
        c = cols_of(g)
        landed(gotx.at[pl.ds(1, 4), :, c], recv.at[KE, g])
        term[2, :, c] += got2p[:, c] + gotx[1, :, c]
        message(term.at[2, :, c], got1p.at[:, c], up, KF, g)
        term[14, :, c] += got2m[:, c] + gotx[4, :, c]
        message(term.at[14, :, c], got1m.at[:, c], down, KF, g)

    def picks():
        for c in loads[1:]:
            c.wait()
        lane, band = iota((BAND, 128), 1), iota((BAND, 128), 0)
        same = iota((128, 128), 0) // BAND == lax.rem(iota((128, 128), 1) // KEEP, 2)
        for i in range(OWN):
            want = jnp.zeros((BAND, 128), jnp.int32)
            for k in range(KEEP):
                want = jnp.where(lax.rem(lane, KEEP) == k, bands[i, k], want)
            onehot = (want == band).astype(BF16)
            for t, wa, wb in ((0, wa_hi, wb_hi), (1, wa_lo, wb_lo)):
                w = jnp.dot(tab[t], onehot, preferred_element_type=F32)
                w = jnp.where(same, w, 0.0).astype(BF16)
                wa[i * 128 : (i + 1) * 128, :] = w
                wb[:, i * 128 : (i + 1) * 128] = w

    def spread(coefs):
        hi, lo = split(by_row(coefs))
        nt = (((1,), (1,)), ((), ()))
        out = lax.dot_general(hi, wb_hi[...], nt, preferred_element_type=F32)
        out += lax.dot_general(hi, wb_lo[...], nt, preferred_element_type=F32)
        out += lax.dot_general(lo, wb_hi[...], nt, preferred_element_type=F32)
        return unstacked(out)

    held = {}

    def step_f(g):
        c = cols_of(g)
        landed(gotx.at[pl.ds(0, 3), :, c], recv.at[KF, g])
        grad = (term[0, :, c] + gotx[0, :, c]) + (got1p[:, c] + got1m[:, c])
        moved = DECAY * momentum[0, :, c] + grad
        hi, lo = split(by_row(stacked(moved)))
        coefs = jnp.dot(hi, wa_hi[...], preferred_element_type=F32)
        coefs += jnp.dot(hi, wa_lo[...], preferred_element_type=F32)
        coefs += jnp.dot(lo, wa_hi[...], preferred_element_type=F32)
        coefs = own_lanes(coefs)
        dense = coefs[0:OWN]
        for j in range(1, TILES):
            dense += coefs[j * OWN : (j + 1) * OWN]
        pair[core, g] = dense
        held[g] = moved, coefs

    def finish_momentum(g):
        moved, coefs = held.pop(g)
        new_momentum[0, :, cols_of(g)] = moved - spread(coefs)

    def rep_message(ref, device, kind, b):
        pltpu.make_async_remote_copy(
            src_ref=ref, dst_ref=ref, send_sem=rep_send.at[kind], recv_sem=rep_recv.at[kind, b],
            device_id=device, device_id_type=MESH,
        ).start()

    def pair_sends(b):
        g0, g1 = BATCHES[b]
        rep_message(pair.at[core, pl.ds(g0, g1 - g0)], beside, 0, b)

    def ring_sends(b):
        g0, g1 = BATCHES[b]
        landed(pair.at[0, pl.ds(g0, g1 - g0)], rep_recv.at[0, b])
        s = slice(g0, g1)
        ring[chip, s] = pair[0, s] + pair[1, s]
        for d in others:
            rep_message(ring.at[chip, pl.ds(g0, g1 - g0)], d, 1, b)

    def weights(b):
        g0, g1 = BATCHES[b]
        landed(ring.at[pl.ds(0, CHIPS - 1), pl.ds(g0, g1 - g0)], rep_recv.at[1, b])
        rows = []
        for g in range(g0, g1):
            total = ring[0, g]
            for k in range(1, CHIPS):
                total += ring[k, g]
            rows += [total * (1.0 / 32)] * TILES
        update = spread(own_lanes(jnp.concatenate(rows, axis=0)))
        c = pl.ds(g0 * GROUP, (g1 - g0) * GROUP)
        new_weight[:, c] = weight[:, c] - STEP_SIZE * update

    loads[0].wait()
    products(0)
    enter()
    first_sends(0)
    x_one(0)
    answer()
    for g in range(1, GROUPS):
        products(g)
        first_sends(g)
        if g < 4:
            x_one(g)
    events = (
        [(3.7 + 2 * g, step_b, g) for g in range(GROUPS)]
        + [(4.7 + 2 * g, step_c, g, K3F) for g in range(GROUPS)]
        + [(12.8, x_one, 4), (16.9, picks)]
        + [(17.0 + 1.3 * g, step_d, g, KXF) for g in range(GROUPS)]
        + [(19.0 + 1.3 * g, step_c, g, K3D) for g in range(GROUPS)]
        + [(27.05, x_one, 5), (27.1, x_one, 6)]
        + [(28 + g, step_d, g, KXD) for g in range(GROUPS)]
        + [(28.1 + g, x_zero, g) for g in range(GROUPS)]
        + [(35 + g, step_e, g) for g in range(GROUPS)]
        + [(42.4, all_there)]
        + [(42.5 + g, step_f, g) for g in range(GROUPS)]
        + [(42.55 + g1 - 1, pair_sends, b) for b, (_, g1) in enumerate(BATCHES)]
        + [(42.6 + g, finish_momentum, g) for g in range(GROUPS)]
        + [(45.58, ring_sends, 0), (48.56, ring_sends, 1), (48.9, ring_sends, 2)]
        + [(49 + b, weights, b) for b in range(len(BATCHES))]
    )
    for _, f, *args in sorted(events, key=lambda e: e[0]):
        f(*args)
    landed(term.at[pl.ds(0, 15)], send.at[0])
    landed(pair.at[0], rep_send.at[0])
    landed(ring.at[pl.ds(0, CHIPS - 1)], rep_send.at[1])


def hand_out(weight, momentum, new_weight, new_momentum, sem):
    copies = [
        pltpu.make_async_copy(weight, new_weight, sem.at[0]),
        pltpu.make_async_copy(momentum, new_momentum, sem.at[1]),
    ]
    for c in copies:
        c.start()
    for c in copies:
        c.wait()


def on_device(acts, cotangent, weight, momentum, bands):
    hbm = pl.BlockSpec(memory_space=pltpu.HBM)
    vmem = pl.BlockSpec(memory_space=pltpu.VMEM)
    unit = lambda *lead: pltpu.VMEM((*lead, OWN, COLS), F32)
    dma = lambda *shape: pltpu.SemaphoreType.DMA(shape)
    results = pl.pallas_call(
        kernel,
        out_shape=(pltpu.VMEM((OWN, COLS), F32), pltpu.VMEM((1, OWN, COLS), F32)),
        in_specs=[hbm] * 6,
        out_specs=(vmem, vmem),
        scratch_shapes=[
            pltpu.SMEM((OWN, KEEP), jnp.int32),
            pltpu.VMEM((ROWS, TOK), BF16),
            pltpu.VMEM((TOK, COLS), BF16),
            unit(), unit(1),
            pltpu.VMEM((2, 2 * BAND, BAND), BF16),
            unit(16), unit(2), unit(2), unit(2), unit(5), unit(), unit(), unit(), unit(),
            pltpu.VMEM((OWN * 128, 128), BF16), pltpu.VMEM((OWN * 128, 128), BF16),
            pltpu.VMEM((128, OWN * 128), BF16), pltpu.VMEM((128, OWN * 128), BF16),
            pltpu.VMEM((2, GROUPS, OWN, 128), F32), pltpu.VMEM((CHIPS, GROUPS, OWN, 128), F32),
            dma(5), dma(GROUPS), dma(7, GROUPS), dma(1), dma(2, len(BATCHES)), dma(2), pltpu.SemaphoreType.REGULAR((2,)),
        ],
        compiler_params=pltpu.CompilerParams(
            collective_id=0, has_side_effects=True, vmem_limit_bytes=40 * 2**20
        ),
    )(*(pltpu.with_memory_space_constraint(a, pltpu.HBM) for a in (bands, acts.T, cotangent, weight, momentum, jnp.asarray(table()))))
    return pl.pallas_call(
        hand_out,
        out_shape=(
            jax.ShapeDtypeStruct((OWN, COLS), F32),
            jax.ShapeDtypeStruct((1, OWN, COLS), F32),
        ),
        in_specs=[pl.BlockSpec(memory_space=pl.ANY)] * 2,
        out_specs=(hbm, hbm),
        scratch_shapes=[dma(2)],
        compiler_params=pltpu.CompilerParams(vmem_limit_bytes=2**20),
    )(*(pltpu.with_memory_space_constraint(a, pltpu.VMEM) for a in results))


def solution(mesh):
    placed = (
        P(("rep", "fsdp"), None),
        P(("rep", "fsdp"), None),
        P("fsdp", None),
        P("rep", "fsdp", None),
        P("fsdp", None),
    )
    return jax.shard_map(
        on_device,
        mesh=mesh,
        in_specs=placed,
        out_specs=(P("fsdp", None), P("rep", "fsdp", None)),
        check_vma=False,
    )
```

```python
import jax
import jax.numpy as jnp
import numpy as np
from jax import lax
from jax.experimental import pallas as pl
from jax.experimental.pallas import tpu as pltpu
from jax.sharding import PartitionSpec as P

MESH = pl.DeviceIdType.MESH
F32, BF16 = jnp.float32, jnp.bfloat16

TOK, COLS, ROWS, BAND, KEEP = 128, 14336, 64, 64, 4
NY = 8
CHIPS = 16
FARTHEST_FIRST = (8, 9, 7, 6, 10, 5, 11, 4, 12, 3, 13, 2, 14, 1, 15)
OWN = 4
OWNERS = ROWS // OWN
GROUP = 2048
GROUPS = COLS // GROUP
HALF = GROUP // 2
CHUNK = 512
TILES = GROUP // 128
BATCHES = [(0, 2), (2, 4), (4, 6), (6, 7)]

STEP_SIZE = 2.0
DECAY = 0.999


def table():
    band, place = np.arange(BAND)[None, :], np.arange(2 * BAND)[:, None] % BAND
    scale = np.where(band == 0, np.sqrt(1.0 / BAND), np.sqrt(2.0 / BAND))
    full = (scale * np.cos(np.pi * (2 * place + 1) * band / (2 * BAND))).astype(np.float32)
    high = full.astype(jnp.bfloat16)
    low = (full - high.astype(np.float32)).astype(jnp.bfloat16)
    return np.stack([high, low])


def cols_of(g, half=None):
    if half is None:
        return pl.ds(g * GROUP, GROUP)
    return pl.ds(g * GROUP + half * HALF, HALF)


def split(x):
    high = x.astype(BF16)
    return high, (x - high.astype(F32)).astype(BF16)


def iota(shape, axis):
    return lax.broadcasted_iota(jnp.int32, shape, axis)


def by_row(x):
    row = lax.rem(iota(x.shape, 0), OWN)
    return jnp.concatenate([jnp.where(row == i, x, 0.0) for i in range(OWN)], axis=1)


def own_lanes(x):
    tile = lax.rem(iota(x.shape, 0) // OWN, TILES)
    return jnp.where(tile == iota(x.shape, 1) // (2 * KEEP), x, 0.0)


def stacked(x):
    return jnp.concatenate([x[:, j * 128 : (j + 1) * 128] for j in range(x.shape[1] // 128)], axis=0)


def unstacked(x):
    return jnp.concatenate([x[j * OWN : (j + 1) * OWN] for j in range(x.shape[0] // OWN)], axis=1)


def kernel(
    bands_hbm, acts_hbm, cot_hbm, weight_hbm, momentum_hbm, table_hbm,
    new_weight, new_momentum,
    bands, acts, cot, weight, momentum, tab,
    term, got4, got3p, got3m, gotx, got2p, got2m, got1p, got1m,
    wa, wb, kept, pair, ring,
    load_sem, cot_sem, recv, send, rep_recv, rep_send, there,
):
    rep, fsdp = lax.axis_index("rep"), lax.axis_index("fsdp")
    chip, core = rep // 2, lax.rem(rep, 2)
    xhi, y = fsdp // NY, lax.rem(fsdp, NY)

    up = (rep, xhi * NY + lax.rem(y + 1, NY))
    down = (rep, xhi * NY + lax.rem(y + NY - 1, NY))
    across = (rep, (1 - xhi) * NY + y)
    beside = (2 * chip + (1 - core), fsdp)
    others = [(2 * lax.rem(chip + t, CHIPS) + core, fsdp) for t in FARTHEST_FIRST]

    loads = [
        pltpu.make_async_copy(src, dst, load_sem.at[i])
        for i, (src, dst) in enumerate(
            [(acts_hbm, acts), (table_hbm, tab), (momentum_hbm, momentum), (weight_hbm, weight), (bands_hbm, bands)]
        )
    ]
    cots = [
        pltpu.make_async_copy(cot_hbm.at[:, c], cot.at[:, c], cot_sem.at[i])
        for i, c in enumerate([cols_of(0, 0), *map(cols_of, range(1, GROUPS)), cols_of(0, 1)])
    ]
    loads[0].start()
    for c in (cots[0], cots[GROUPS], *cots[1:GROUPS]):
        c.start()
    for c in loads[1:]:
        c.start()

    barrier = pltpu.get_barrier_semaphore()
    for d in (up, down, across):
        pl.semaphore_signal(barrier, inc=1, device_id=d, device_id_type=MESH)

    def tell(sem, first, last):
        @pl.loop(first, last)
        def _(i):
            pl.semaphore_signal(sem, inc=1, device_id=(2 * i + core, fsdp), device_id_type=MESH)

    tell(barrier, chip + 1, CHIPS)

    @pl.when(core == 0)
    def _():
        pl.semaphore_signal(barrier, inc=1, device_id=beside, device_id_type=MESH)

    def enter():
        pl.semaphore_wait(barrier, 3 + chip + core)

    def answer():
        tell(there.at[0], 0, chip)

        @pl.when(core == 1)
        def _():
            pl.semaphore_signal(there.at[1], inc=1, device_id=beside, device_id_type=MESH)

    def all_there():
        @pl.when(core == 0)
        def _():
            pl.semaphore_wait(there.at[1], 1)

        @pl.when(chip < CHIPS - 1)
        def _():
            pl.semaphore_wait(there.at[0], CHIPS - 1 - chip)

    def message(src, dst, device, kind, g):
        pltpu.make_async_remote_copy(
            src_ref=src, dst_ref=dst, send_sem=send.at[0], recv_sem=recv.at[kind, g],
            device_id=device, device_id_type=MESH,
        ).start()

    def landed(ref, sem):
        pltpu.make_async_copy(ref, ref, sem).wait()

    K4, K3F, K3D, KXF, KXD, KE, KF = range(7)

    def products(g, half):
        if half == 0 or g == 0:
            cots[g if half == 0 else GROUPS].wait()
        for s in range(HALF // CHUNK):
            at = pl.ds(g * GROUP + half * HALF + s * CHUNK, CHUNK)
            out = jnp.dot(acts[...], cot[:, at], preferred_element_type=F32)
            for o in range(OWNERS):
                r = xhi if o < NY else 1 - xhi
                u = 2 * lax.rem(o % NY - y + NY, NY) + r
                term[u, :, at] = out[o * OWN : (o + 1) * OWN]

    def first_sends(g, half):
        c = cols_of(g, half)
        if half == 0:
            message(term.at[pl.ds(8, 2), :, c], got4.at[:, :, c], up, K4, g)
            message(term.at[pl.ds(10, 2), :, c], got3m.at[:, :, c], down, K3F, g)
        else:
            message(term.at[pl.ds(8, 2), :, c], got4.at[:, :, c], down, K4, g)
            message(term.at[pl.ds(6, 2), :, c], got3p.at[:, :, c], up, K3F, g)

    def x_one(g):
        c = cols_of(g)
        message(term.at[3, :, c], gotx.at[1, :, c], across, KE, g)
        message(term.at[15, :, c], gotx.at[4, :, c], across, KE, g)

    def x_zero(g):
        c = cols_of(g)
        message(term.at[1, :, c], gotx.at[0, :, c], across, KF, g)

    def step_b(g):
        e, o = cols_of(g, 0), cols_of(g, 1)
        landed(got4.at[:, :, cols_of(g)], recv.at[K4, g])
        term[6:8, :, e] += got4[:, :, e]
        message(term.at[pl.ds(6, 2), :, e], got3p.at[:, :, e], up, K3D, g)
        term[10:12, :, o] += got4[:, :, o]
        message(term.at[pl.ds(10, 2), :, o], got3m.at[:, :, o], down, K3D, g)

    def step_c(g, kind):
        landed(got3p.at[:, :, cols_of(g)], recv.at[kind, g])
        then = KXF if kind == K3F else KXD
        c = cols_of(g, 1 if kind == K3F else 0)
        term[5, :, c] += got3p[1, :, c]
        message(term.at[5, :, c], gotx.at[2, :, c], across, then, g)
        term[4, :, c] += got3p[0, :, c]
        c = cols_of(g, 0 if kind == K3F else 1)
        term[13, :, c] += got3m[1, :, c]
        message(term.at[13, :, c], gotx.at[3, :, c], across, then, g)
        term[12, :, c] += got3m[0, :, c]

    def step_d(g, kind):
        landed(gotx.at[pl.ds(2, 2), :, cols_of(g, 0)], recv.at[kind, g])
        c = cols_of(g, 1 if kind == KXF else 0)
        term[4, :, c] += gotx[2, :, c]
        message(term.at[4, :, c], got2p.at[:, c], up, KE, g)
        c = cols_of(g, 0 if kind == KXF else 1)
        term[12, :, c] += gotx[3, :, c]
        message(term.at[12, :, c], got2m.at[:, c], down, KE, g)

    def step_e(g):
        c = cols_of(g)
        landed(gotx.at[pl.ds(1, 4), :, c], recv.at[KE, g])
        term[2, :, c] += got2p[:, c] + gotx[1, :, c]
        message(term.at[2, :, c], got1p.at[:, c], up, KF, g)
        term[14, :, c] += got2m[:, c] + gotx[4, :, c]
        message(term.at[14, :, c], got1m.at[:, c], down, KF, g)

    def picks():
        for c in loads[1:]:
            c.wait()
        lane, band = iota((BAND, 128), 1), iota((BAND, 128), 0)
        same = iota((128, 128), 0) // BAND == lax.rem(iota((128, 128), 1) // KEEP, 2)
        for i in range(OWN):
            want = jnp.zeros((BAND, 128), jnp.int32)
            for k in range(KEEP):
                want = jnp.where(lax.rem(lane, KEEP) == k, bands[i, k], want)
            onehot = (want == band).astype(BF16)
            for t, places in ((0, (0, 2)), (1, (1,))):
                w = jnp.dot(tab[t], onehot, preferred_element_type=F32)
                w = jnp.where(same, w, 0.0).astype(BF16)
                for p in places:
                    at = slice((p * OWN + i) * 128, (p * OWN + i + 1) * 128)
                    wa[at, :] = w
                    wb[:, at] = w

    def spread(coefs):
        hi, lo = split(by_row(coefs))
        nt = (((1,), (1,)), ((), ()))
        out = lax.dot_general(
            jnp.concatenate([hi, hi, lo], axis=1), wb[...], nt, preferred_element_type=F32
        )
        return unstacked(out)

    def step_f(g):
        c = cols_of(g)
        landed(gotx.at[pl.ds(0, 3), :, c], recv.at[KF, g])
        grad = (term[0, :, c] + gotx[0, :, c]) + (got1p[:, c] + got1m[:, c])
        moved = DECAY * momentum[0, :, c] + grad
        hi, lo = split(by_row(stacked(moved)))
        coefs = own_lanes(
            jnp.dot(jnp.concatenate([hi, hi, lo], axis=1), wa[...], preferred_element_type=F32)
        )
        dense = coefs[0:OWN]
        for j in range(1, TILES):
            dense += coefs[j * OWN : (j + 1) * OWN]
        pair[core, g] = dense
        kept[g] = coefs
        new_momentum[0, :, c] = moved

    def finish_momentum(g0, g1):
        c = pl.ds(g0 * GROUP, (g1 - g0) * GROUP)
        coefs = kept[g0:g1].reshape((g1 - g0) * OWN * TILES, 128)
        new_momentum[0, :, c] -= spread(coefs)

    def rep_message(ref, device, kind, b):
        pltpu.make_async_remote_copy(
            src_ref=ref, dst_ref=ref, send_sem=rep_send.at[kind], recv_sem=rep_recv.at[kind, b],
            device_id=device, device_id_type=MESH,
        ).start()

    def pair_sends(b):
        g0, g1 = BATCHES[b]
        rep_message(pair.at[core, pl.ds(g0, g1 - g0)], beside, 0, b)

    def ring_sends(b):
        g0, g1 = BATCHES[b]
        landed(pair.at[0, pl.ds(g0, g1 - g0)], rep_recv.at[0, b])
        s = slice(g0, g1)
        ring[chip, s] = pair[0, s] + pair[1, s]
        for d in others:
            rep_message(ring.at[chip, pl.ds(g0, g1 - g0)], d, 1, b)

    def weights(b):
        g0, g1 = BATCHES[b]
        landed(ring.at[pl.ds(0, CHIPS - 1), pl.ds(g0, g1 - g0)], rep_recv.at[1, b])
        rows = []
        for g in range(g0, g1):
            total = ring[0, g]
            for k in range(1, CHIPS):
                total += ring[k, g]
            rows += [total * (1.0 / 32)] * TILES
        update = spread(own_lanes(jnp.concatenate(rows, axis=0)))
        c = pl.ds(g0 * GROUP, (g1 - g0) * GROUP)
        new_weight[:, c] = weight[:, c] - STEP_SIZE * update

    loads[0].wait()
    products(0, 0)
    enter()
    first_sends(0, 0)
    products(0, 1)
    first_sends(0, 1)
    x_one(0)
    answer()
    for g in range(1, GROUPS):
        for half in range(2):
            products(g, half)
            first_sends(g, half)
        if g < 4:
            x_one(g)
    events = (
        [(3.7 + 2 * g, step_b, g) for g in range(GROUPS)]
        + [(4.7 + 2 * g, step_c, g, K3F) for g in range(GROUPS)]
        + [(12.8, x_one, 4), (16.9, picks)]
        + [(17.0 + 1.3 * g, step_d, g, KXF) for g in range(GROUPS)]
        + [(19.0 + 1.3 * g, step_c, g, K3D) for g in range(GROUPS)]
        + [(27.05, x_one, 5), (27.1, x_one, 6)]
        + [(28 + g, step_d, g, KXD) for g in range(GROUPS)]
        + [(28.1 + g, x_zero, g) for g in range(GROUPS)]
        + [(35 + g, step_e, g) for g in range(GROUPS)]
        + [(42.4, all_there)]
        + [(42.5 + g, step_f, g) for g in range(GROUPS)]
        + [(42.55 + g1 - 1, pair_sends, b) for b, (_, g1) in enumerate(BATCHES)]
        + [(48.91, finish_momentum, 0, 4), (48.92, finish_momentum, 4, GROUPS)]
        + [(44.58, ring_sends, 0), (46.58, ring_sends, 1), (48.56, ring_sends, 2), (48.9, ring_sends, 3)]
        + [(49 + b, weights, b) for b in range(len(BATCHES))]
    )
    for _, f, *args in sorted(events, key=lambda e: e[0]):
        f(*args)
    landed(term.at[pl.ds(0, 15)], send.at[0])
    landed(pair.at[0], rep_send.at[0])
    landed(ring.at[pl.ds(0, CHIPS - 1)], rep_send.at[1])


def hand_out(weight, momentum, new_weight, new_momentum, sem):
    copies = [
        pltpu.make_async_copy(weight, new_weight, sem.at[0]),
        pltpu.make_async_copy(momentum, new_momentum, sem.at[1]),
    ]
    for c in copies:
        c.start()
    for c in copies:
        c.wait()


def on_device(acts, cotangent, weight, momentum, bands):
    hbm = pl.BlockSpec(memory_space=pltpu.HBM)
    vmem = pl.BlockSpec(memory_space=pltpu.VMEM)
    unit = lambda *lead: pltpu.VMEM((*lead, OWN, COLS), F32)
    dma = lambda *shape: pltpu.SemaphoreType.DMA(shape)
    results = pl.pallas_call(
        kernel,
        out_shape=(pltpu.VMEM((OWN, COLS), F32), pltpu.VMEM((1, OWN, COLS), F32)),
        in_specs=[hbm] * 6,
        out_specs=(vmem, vmem),
        scratch_shapes=[
            pltpu.SMEM((OWN, KEEP), jnp.int32),
            pltpu.VMEM((ROWS, TOK), BF16),
            pltpu.VMEM((TOK, COLS), BF16),
            unit(), unit(1),
            pltpu.VMEM((2, 2 * BAND, BAND), BF16),
            unit(16), unit(2), unit(2), unit(2), unit(5), unit(), unit(), unit(), unit(),
            pltpu.VMEM((3 * OWN * 128, 128), BF16), pltpu.VMEM((128, 3 * OWN * 128), BF16),
            pltpu.VMEM((GROUPS, OWN * TILES, 128), F32),
            pltpu.VMEM((2, GROUPS, OWN, 128), F32), pltpu.VMEM((CHIPS, GROUPS, OWN, 128), F32),
            dma(5), dma(GROUPS + 1), dma(7, GROUPS), dma(1), dma(2, len(BATCHES)), dma(2), pltpu.SemaphoreType.REGULAR((2,)),
        ],
        compiler_params=pltpu.CompilerParams(
            collective_id=0, has_side_effects=True, vmem_limit_bytes=40 * 2**20
        ),
    )(*(pltpu.with_memory_space_constraint(a, pltpu.HBM) for a in (bands, acts.T, cotangent, weight, momentum, jnp.asarray(table()))))
    return pl.pallas_call(
        hand_out,
        out_shape=(
            jax.ShapeDtypeStruct((OWN, COLS), F32),
            jax.ShapeDtypeStruct((1, OWN, COLS), F32),
        ),
        in_specs=[pl.BlockSpec(memory_space=pl.ANY)] * 2,
        out_specs=(hbm, hbm),
        scratch_shapes=[dma(2)],
        compiler_params=pltpu.CompilerParams(vmem_limit_bytes=2**20),
    )(*(pltpu.with_memory_space_constraint(a, pltpu.VMEM) for a in results))


def solution(mesh):
    placed = (
        P(("rep", "fsdp"), None),
        P(("rep", "fsdp"), None),
        P("fsdp", None),
        P("rep", "fsdp", None),
        P("fsdp", None),
    )
    return jax.shard_map(
        on_device,
        mesh=mesh,
        in_specs=placed,
        out_specs=(P("fsdp", None), P("rep", "fsdp", None)),
        check_vma=False,
    )
```
